32 devices in a mesh: rep: 8 (over z, x), shard: 4 (over y, core).
Axes of the slice: x: 2, y: 2, z: 4, core: 2. Of those that a mesh axis runs over, the one named last changes fastest.
Arguments:
- tokens: bfloat16 [16384, 768], P(('rep', 'shard')), may hold values from -6 to 6
- cotangent: bfloat16 [16384, 768], P(('rep', 'shard')), may hold values from -6 to 6
- lengths: int32 [32, 4], P(('rep', 'shard')), may hold values from 0 to 512, as said below
- routes: int32 [2, 16384, 1], P(None, ('rep', 'shard')), may hold values from 0 to 1; in each aligned block of 512 rows (0 to 511, 512 to 1023, ..., all dimensions but the last counted through in order) at most 288 rows name the same one
- buckets: int32 [1023], replicated, may hold values from 0 to 31, as said below
- w_qkv: bfloat16 [2, 3, 768, 768], P(None, None, 'shard'), may hold values from -0.21875 to 0.21875
- w_attn_out: bfloat16 [2, 768, 768], P(None, 'shard'), may hold values from -0.875 to 0.875
- gains: bfloat16 [2, 2, 768], P(None, None, 'shard'), may hold values from 0.5 to 1.5
- router: bfloat16 [2, 768, 2], P(None, 'shard'), may hold values from -0.15625 to 0.15625
- w_in: bfloat16 [2, 2, 768, 3072], P(None, None, 'shard'), may hold values from -0.21875 to 0.21875
- w_out: bfloat16 [2, 2, 3072, 768], P(None, None, 'shard'), may hold values from -0.21875 to 0.21875
- bias_table: bfloat16 [32, 12], P('shard'), may hold values from -4 to 4
Outputs:
- out_tokens: bfloat16 [16384, 768], P(('rep', 'shard'))
- grad_tokens: float32 [16384, 768], P(('rep', 'shard'))
- grad_w_qkv: float32 [2, 3, 768, 768], P(None, None, 'shard')
- grad_w_attn_out: float32 [2, 768, 768], P(None, 'shard')
- grad_gains: float32 [2, 2, 768], P(None, None, 'shard')
- grad_router: float32 [2, 768, 2], P(None, 'shard')
- grad_w_in: float32 [2, 2, 768, 3072], P(None, None, 'shard')
- grad_w_out: float32 [2, 2, 3072, 768], P(None, None, 'shard')
- grad_bias_table: float32 [32, 12], P('shard')
The draws below stay inside these ranges and needn't reach their ends.
Inputs may be any that keep to these rules, and one draw needn't show every extreme that they name: Each device's lengths sum to at most 512; one device holds a single sequence of 512 rows. `routes`: in each layer the rows of one device name each expert at most 288 times. buckets[511 + r] is 0 for r = 0, never falls as |r| grows on either side, is below 16 for r <= 0 and 16 or more for r > 0.
All inputs are finite; a program needn't handle non-finite values.
Results may differ from the reference program's by a relative error of at most 0.029.
Values may be sent and summed in bfloat16 or wider, within the bound.
A program may use at most 320 MiB of HBM per device.

```python
import math
import jax
import jax.numpy as jnp
import numpy as np
from jax import lax

D = 768
H = 12
DH = 64
FF = 3072
NB = 32
E = 2
LAYERS = 2
SEQ_DEV = 4
TOK_DEV = 512
CAP = 288
TOKENS = 16384
DEVICES = 32


def draw_lengths(key, part):
    key = jax.random.fold_in(key, 11)
    fill_key, cut_key, pick_key = jax.random.split(key, 3)
    fills = jax.random.randint(fill_key, (DEVICES, 1), TOK_DEV // 2, TOK_DEV + 1).astype(jnp.int32)
    cuts = jax.random.randint(cut_key, (DEVICES, SEQ_DEV - 1), 0, TOK_DEV + 1).astype(jnp.int32)
    cuts = jnp.sort(jnp.minimum(cuts, fills), axis=1)
    chosen = jax.random.randint(pick_key, (), 0, DEVICES)
    whole = jnp.arange(DEVICES)[:, None] == chosen
    fills = jnp.where(whole, TOK_DEV, fills).astype(jnp.int32)
    cuts = jnp.where(whole, TOK_DEV, cuts).astype(jnp.int32)
    edges = jnp.concatenate([jnp.zeros((DEVICES, 1), jnp.int32), cuts, fills], axis=1)
    return (edges[:, 1:] - edges[:, :-1]).astype(jnp.int32)


def draw_buckets(key, part):
    key = jax.random.fold_in(key, 7)
    half = NB // 2
    picks = jax.random.permutation(key, TOK_DEV - 1)[:half - 1] + 1
    bounds = jnp.sort(picks.astype(jnp.int32))
    offsets = jnp.arange(2 * TOK_DEV - 1, dtype=jnp.int32) - (TOK_DEV - 1)
    distance = jnp.abs(offsets)
    base = jnp.sum((distance[:, None] >= bounds[None, :]).astype(jnp.int32), axis=1)
    return (base + jnp.where(offsets > 0, half, 0)).astype(jnp.int32)


def block_levels(rng, dims, cuts, smallest, top_value):
    gain, own = 1.0, jax.random.fold_in(rng, 6)
    for dim, parts in cuts:
        draws = jnp.exp(jax.random.uniform(jax.random.fold_in(own, dim), (parts,), jnp.float32, smallest / len(cuts), top_value / len(cuts)))
        gain = gain * jnp.repeat(draws, dims[dim] // parts).reshape([-1 if axis == dim else 1 for axis in range(len(dims))])
    return gain


def deal_out(rng, own, number, rows, amount, top, bound, slope):
    ranking = jax.random.permutation(rng, amount)
    packed, ordinary = shares(amount, rows * top, bound, slope, True), shares(amount, rows * top, bound, slope, False)
    places = jnp.arange(amount)

    def named(sizes, turn):
        used = int((sizes > 0).sum())
        fixed = max(1, used // 4)
        passed = fixed + (places - fixed + turn * (used - fixed)) % max(1, amount - fixed)
        return jnp.zeros((amount,), jnp.int32).at[ranking[jnp.where(places < fixed, places, passed)]].set(jnp.asarray(sizes, jnp.int32))

    sizes = jnp.where(number % 4 == 0, named(packed, number // 4), named(ordinary, number - number // 4 - 1))
    mixed = jax.random.permutation(jax.random.fold_in(own, 3), amount)
    source_of, taker = mixed[0:amount // 2 * 2:2], mixed[1:amount // 2 * 2:2]
    margin = jnp.minimum(sizes[source_of] - 1, bound - sizes[taker]) // 2
    margin = jnp.where((source_of == ranking[0]) | (taker == ranking[0]) | (sizes[taker] == 0), 0, jnp.maximum(margin, 0))
    passed = jax.random.randint(jax.random.fold_in(own, 4), (amount // 2,), 0, 1 << 20) % (margin + 1)
    sizes = sizes.at[source_of].add(-passed).at[taker].add(passed)
    labels = jnp.searchsorted(jnp.cumsum(sizes), jnp.arange(rows * top), side="right").astype(jnp.int32)
    table = labels.reshape(top, rows).T
    table = table[jax.random.permutation(jax.random.fold_in(own, 1), rows)]
    turn = jax.random.randint(jax.random.fold_in(own, 2), (rows, 1), 0, top)
    return jnp.take_along_axis(table, (jnp.arange(top)[None, :] + turn) % top, axis=1)


def shares(number_of, total, most, skew, full):
    weights = [(1 << 20) // math.isqrt(standing ** skew) + 1 for standing in range(1, number_of + 1)]
    largest = most if full else min(most, max(-(-total // number_of), total * weights[0] // sum(weights)))
    least = 1 if total - largest >= number_of - 1 else 0
    counts, rest = [largest] + [least] * (number_of - 1), total - largest - least * (number_of - 1)
    while rest > 0:
        candidates = [i for i in range(1, number_of) if counts[i] < largest] or [i for i in range(1, number_of) if counts[i] < most]
        pool, budget = sum([weights[i] for i in candidates]), rest
        for i in candidates:
            addition = min(most - counts[i], max(1, budget * weights[i] // pool), rest)
            counts[i] = counts[i] + addition
            rest = rest - addition
    return np.array(counts)


def scatter_about(key, extent, deviation, reach, cuts=(), kind=jnp.bfloat16):
    entries = deviation * jax.random.normal(key, extent, jnp.float32)
    if cuts:
        entries = entries * block_levels(key, extent, cuts, -0.22, 0.18)
    return jnp.clip(entries, -reach, reach).astype(kind)


def setup_inputs(seed: int = 0) -> dict:
    splits = jax.random.split(jax.random.key(seed), 13)
    tokens = scatter_about(splits[0], (TOKENS, D), 1.0, 6.0, ((0, 32),))
    cotangent = scatter_about(splits[1], (TOKENS, D), 1.0, 6.0, ((0, 32),))
    lengths = draw_lengths(jax.random.fold_in(splits[12], 71), 0)
    routes_keys = jax.random.split(jax.random.fold_in(splits[3], 1), LAYERS * TOKENS // TOK_DEV)
    routes_turns = jax.random.permutation(jax.random.fold_in(splits[3], 3), LAYERS * TOKENS // TOK_DEV)
    routes = jax.vmap(lambda own, number: deal_out(jax.random.fold_in(splits[3], 2), own, number, TOK_DEV, E, 1, CAP, 1))(routes_keys, routes_turns).reshape((LAYERS, TOKENS, 1))
    buckets = draw_buckets(jax.random.fold_in(splits[12], 71), 0)
    w_qkv = scatter_about(splits[5], (LAYERS, 3, D, D), D ** -0.5, 0.21875, ((2, 4),))
    w_attn_out = scatter_about(splits[6], (LAYERS, D, D), (D // 16) ** -0.5, 0.875, ((1, 4),))
    gains = jnp.clip(1.0 + 0.1 * jax.random.normal(splits[7], (LAYERS, 2, D), jnp.float32), 0.5, 1.5).astype(jnp.bfloat16)
    router = scatter_about(splits[8], (LAYERS, D, E), (2 * D) ** -0.5, 0.15625, ((1, 4),))
    w_in = scatter_about(splits[9], (LAYERS, E, D, FF), D ** -0.5, 0.21875, ((2, 4),))
    w_out = scatter_about(splits[10], (LAYERS, E, FF, D), (FF // 4) ** -0.5, 0.21875, ((2, 4),))
    bias_table = scatter_about(splits[11], (NB, H), 0.8, 4.0, ((0, 4),))
    return {"tokens": tokens, "cotangent": cotangent, "lengths": lengths, "routes": routes, "buckets": buckets, "w_qkv": w_qkv, "w_attn_out": w_attn_out, "gains": gains, "router": router, "w_in": w_in, "w_out": w_out, "bias_table": bias_table}


EPSILON = 1e-06
NEGATIVE = -1e+30
HIGHEST = lax.Precision.HIGHEST

@jax.custom_vjp
def low(v):
    return lax.optimization_barrier(v.astype(jnp.bfloat16)).astype(jnp.float32)

@jax.custom_vjp
def low_back(v):
    return v

def low_keep(v):
    return (low(v), None)

def low_pass(kept, grad):
    return (grad,)

def back_keep(v):
    return (v, None)

def back_low(kept, grad):
    return (low(grad),)
low.defvjp(low_keep, low_pass)
low_back.defvjp(back_keep, back_low)

def rounded_both(value):
    return low_back(low(value))

def inverse_rms(hidden):
    return lax.rsqrt(lax.optimization_barrier(jnp.mean(hidden * hidden, axis=1, keepdims=True)) + EPSILON)

def attention(queries, keys, values, rel_rows, segment):
    total = queries.shape[0]
    query_heads = queries.reshape(total, H, DH)
    key_heads = keys.reshape(total, H, DH)
    value_heads = values.reshape(total, H, DH)
    scores = jnp.einsum('qhd,khd->hqk', query_heads, key_heads, precision=HIGHEST) * DH ** (-0.5)
    positions = jnp.arange(total, dtype=jnp.int32)
    offsets = positions[None, :] - positions[:, None] + (total - 1)
    scores = low_back(scores + jnp.take(rel_rows, offsets, axis=1))
    same_doc = segment[:, None] == segment[None, :]
    masked = jnp.where(same_doc[None], scores, NEGATIVE)
    highest = lax.optimization_barrier(jnp.max(masked, axis=2, keepdims=True))
    exponent = jnp.exp(masked - highest)
    weights = exponent / lax.optimization_barrier(jnp.sum(exponent, axis=2, keepdims=True))
    mixed = jnp.einsum('hqk,khd->qhd', low(weights), value_heads, precision=HIGHEST)
    return mixed.reshape(total, H * DH)

def encoder_layer(hidden, params, bucket_hot, segment, route):
    qkv_w, out_w, gain_w, route_w, in_w, outer_w, table = params
    experts = in_w.shape[0]
    rel_rows = jnp.dot(bucket_hot, table, precision=HIGHEST).T
    route_hot = (route[:, None] == jnp.arange(experts, dtype=jnp.int32)[None, :]).astype(jnp.int32)
    earlier = (jnp.cumsum(route_hot, axis=0) - route_hot).astype(jnp.int32)
    slot_index = (route * CAP + lax.optimization_barrier(jnp.sum(earlier * route_hot, axis=1))).astype(jnp.int32)
    normed_one = low(hidden * inverse_rms(hidden) * gain_w[0])
    queries = rounded_both(jnp.dot(normed_one, qkv_w[0], precision=HIGHEST))
    keys = rounded_both(jnp.dot(normed_one, qkv_w[1], precision=HIGHEST))
    values = rounded_both(jnp.dot(normed_one, qkv_w[2], precision=HIGHEST))
    attended = rounded_both(attention(queries, keys, values, rel_rows, segment))
    middle = hidden + low_back(jnp.dot(attended, out_w, precision=HIGHEST))
    normed_two = low(middle * inverse_rms(middle) * gain_w[1])
    logits = low_back(jnp.dot(normed_two, route_w, precision=HIGHEST))
    shifted = jnp.exp(logits - lax.optimization_barrier(jnp.max(logits, axis=1, keepdims=True)))
    softmax_w = shifted / lax.optimization_barrier(jnp.sum(shifted, axis=1, keepdims=True))
    gate = lax.optimization_barrier(jnp.sum(softmax_w * route_hot.astype(jnp.float32), axis=1, keepdims=True))
    placed = jnp.zeros((experts * CAP, hidden.shape[1]), jnp.float32).at[slot_index].set(normed_two)
    placed = placed.reshape(experts, CAP, hidden.shape[1])
    upward = low_back(jnp.einsum('ecd,edf->ecf', placed, in_w, precision=HIGHEST))
    active = low(jax.nn.gelu(upward, approximate=True))
    expert_out = rounded_both(jnp.einsum('ecf,efd->ecd', active, outer_w, precision=HIGHEST))
    expert_out = expert_out.reshape(experts * CAP, hidden.shape[1])
    return middle + gate * jnp.take(expert_out, slot_index, axis=0)

def device_pass(hidden, params, lengths_row, route_rows, buckets):
    positions = jnp.arange(hidden.shape[0], dtype=jnp.int32)
    bounds = jnp.cumsum(lengths_row).astype(jnp.int32)
    segment = lax.optimization_barrier(jnp.sum((positions[:, None] >= bounds[None, :]).astype(jnp.int32), axis=1)).astype(jnp.int32)
    bucket_hot = (buckets[:, None] == jnp.arange(NB, dtype=jnp.int32)[None, :]).astype(jnp.float32)
    w_qkv, w_attn_out, gains, router, w_in, w_out, bias_table = params
    for index in range(LAYERS):
        layer_params = (w_qkv[index], w_attn_out[index], gains[index], router[index], w_in[index], w_out[index], bias_table)
        hidden = encoder_layer(hidden, layer_params, bucket_hot, segment, route_rows[index])
    return hidden

def reference(tokens, cotangent, lengths, routes, buckets, w_qkv, w_attn_out, gains, router, w_in, w_out, bias_table):
    params = tuple((weight.astype(jnp.float32) for weight in (w_qkv, w_attn_out, gains, router, w_in, w_out, bias_table)))
    start = tokens.astype(jnp.float32).reshape(DEVICES, TOK_DEV, D)
    route_rows = jnp.transpose(routes[:, :, 0].reshape(LAYERS, DEVICES, TOK_DEV), (1, 0, 2))
    positions = jnp.arange(TOK_DEV, dtype=jnp.int32)
    filled = lax.optimization_barrier(jnp.sum(lengths, axis=1)).astype(jnp.int32)
    live_mask = (positions[None, :] < filled[:, None]).astype(jnp.float32)
    stepper = jax.checkpoint(device_pass)

    def forward(inputs, weights):

        def single(item):
            return stepper(item[0], weights, item[1], item[2], buckets)
        return lax.map(single, (inputs, lengths, route_rows))
    result, pullback = jax.vjp(forward, start, params)
    upstream_grad = cotangent.astype(jnp.float32).reshape(DEVICES, TOK_DEV, D) * live_mask[:, :, None]
    grad_start, grad_params = pullback(upstream_grad)
    return (result.reshape(TOKENS, D).astype(jnp.bfloat16), grad_start.reshape(TOKENS, D), grad_params[0], grad_params[1], grad_params[2], grad_params[3], grad_params[4], grad_params[5], grad_params[6])
```

```python
import functools

import jax
import jax.numpy as jnp
from jax import lax
from jax.experimental import pallas as pl
from jax.experimental.pallas import tpu as pltpu
from jax.sharding import PartitionSpec as P

H = 12
DH = 64
NB = 32
CAP = 288
PAIR = 2 * DH
STRIP = 128

EPSILON = 1e-06
NEGATIVE = -1e30
HIGHEST = lax.Precision.HIGHEST
F32 = jnp.float32
BF16 = jnp.bfloat16


def matmul(a, b, dims=((1,), (0,))):
    return lax.dot_general(a, b, (dims, ((), ())), preferred_element_type=F32)


def inverse_rms(hidden):
    return lax.rsqrt(jnp.mean(hidden * hidden, axis=1, keepdims=True) + EPSILON)


def norm_backward(hidden, scaling, gain_row, upstream):
    weighted = upstream * gain_row
    inner = jnp.sum(weighted * hidden, axis=1, keepdims=True)
    cubed = scaling * scaling * scaling / hidden.shape[1]
    delta_hidden = scaling * weighted - cubed * hidden * inner
    delta_gain = jnp.sum(upstream * hidden * scaling, axis=0)
    return (delta_hidden, delta_gain)


def strip_bias(rel_row, total):
    span = 2 * total
    wide = jnp.broadcast_to(rel_row, (STRIP, span))
    strip = pltpu.roll(wide, span - (STRIP - 1), 1, stride=1, stride_axis=0)
    first = total - STRIP
    return jnp.concatenate(
        [strip[:, first - begin : first - begin + total] for begin in range(0, total, STRIP)],
        axis=0,
    )


def strip_sums(delta_scores, mirror, total):
    span = 2 * total
    first = total - STRIP
    acc = jnp.zeros((STRIP, span), F32)
    for begin in range(0, total, STRIP):
        part = matmul(mirror, delta_scores[begin : begin + STRIP])
        left = first - begin
        pieces = [part, jnp.zeros((STRIP, span - total - left), F32)]
        if left:
            pieces = [jnp.zeros((STRIP, left), F32)] + pieces
        acc = acc + jnp.concatenate(pieces, axis=1)
    skewed = pltpu.roll(acc, 0, 1, stride=1, stride_axis=0)
    return jnp.sum(skewed, axis=0, keepdims=True)


def head_weights(queries, keys, rel_row, same, total):
    scores = matmul(queries, keys, ((1,), (1,))) * DH ** (-0.5) + strip_bias(rel_row, total)
    scores = jnp.where(same, scores, NEGATIVE)
    exponent = jnp.exp(scores - jnp.max(scores, axis=1, keepdims=True))
    return exponent * (1.0 / jnp.sum(exponent, axis=1, keepdims=True))


def forward_kernel(rel_ref, row_seg_ref, col_seg_ref, q_ref, k_ref, v_ref, o_ref):
    total = q_ref.shape[0]
    same = row_seg_ref[...] == col_seg_ref[...]
    low_half = lax.broadcasted_iota(jnp.int32, (total, PAIR), 1) < DH
    q, k, v = q_ref[...], k_ref[...], v_ref[...]
    zero = jnp.zeros_like(q)
    outs = []
    for side in range(2):
        mine = low_half if side == 0 else jnp.logical_not(low_half)
        weights = head_weights(
            jnp.where(mine, q, zero), k, rel_ref[side : side + 1, :], same, total
        )
        outs.append(matmul(weights.astype(BF16), v))
    o_ref[...] = jnp.where(low_half, outs[0], outs[1]).astype(BF16)


def backward_kernel(
    rel_ref, row_seg_ref, col_seg_ref, q_ref, k_ref, v_ref, do_ref, dqkv_ref, drel_ref
):
    total = q_ref.shape[0]
    same = row_seg_ref[...] == col_seg_ref[...]
    low_half = lax.broadcasted_iota(jnp.int32, (total, PAIR), 1) < DH
    mirror = (
        lax.broadcasted_iota(jnp.int32, (STRIP, STRIP), 0)
        + lax.broadcasted_iota(jnp.int32, (STRIP, STRIP), 1)
        == STRIP - 1
    ).astype(F32).astype(BF16)
    q, k, v, do = q_ref[...], k_ref[...], v_ref[...], do_ref[...]
    zero = jnp.zeros_like(q)
    scaling = DH ** (-0.5)
    outs = []
    for side in range(2):
        mine = low_half if side == 0 else jnp.logical_not(low_half)
        weights = head_weights(
            jnp.where(mine, q, zero), k, rel_ref[side : side + 1, :], same, total
        )
        delta_weights = matmul(jnp.where(mine, do, zero), v, ((1,), (1,)))
        inner = jnp.sum(weights * delta_weights, axis=1, keepdims=True)
        delta_scores = (weights * (delta_weights - inner)).astype(BF16)
        outs.append(
            (
                matmul(delta_scores, k) * scaling,
                matmul(delta_scores, q, ((0,), (0,))) * scaling,
                matmul(weights.astype(BF16), do, ((0,), (0,))),
            )
        )
        drel_ref[side : side + 1, :] = strip_sums(delta_scores, mirror, total)
    for index in range(3):
        dqkv_ref[index] = jnp.where(low_half, outs[0][index], outs[1][index]).astype(BF16)


def attention_specs(total):
    rel = pl.BlockSpec((None, 2, 2 * total), lambda i: (i, 0, 0))
    row_seg = pl.BlockSpec((total, 1), lambda i: (0, 0))
    col_seg = pl.BlockSpec((1, total), lambda i: (0, 0))
    qkv = [
        pl.BlockSpec((None, total, PAIR), functools.partial(lambda which, i: (which, 0, i), which))
        for which in range(3)
    ]
    return [rel, row_seg, col_seg] + qkv


def attend_forward(rel_pairs, row_seg, col_seg, qkv):
    total, width = qkv.shape[1:]
    return pl.pallas_call(
        forward_kernel,
        grid=(H // 2,),
        in_specs=attention_specs(total),
        out_specs=pl.BlockSpec((total, PAIR), lambda i: (0, i)),
        out_shape=jax.ShapeDtypeStruct((total, width), BF16),
        compiler_params=pltpu.CompilerParams(vmem_limit_bytes=40 * 2**20),
        cost_estimate=pl.CostEstimate(
            flops=4 * H * total * total * DH * 4, bytes_accessed=8 * total * width,
            transcendentals=H * total * total,
        ),
        name="attend_forward",
    )(rel_pairs, row_seg, col_seg, qkv, qkv, qkv)


def attend_backward(rel_pairs, row_seg, col_seg, qkv, upstream):
    total, width = qkv.shape[1:]
    return pl.pallas_call(
        backward_kernel,
        grid=(H // 2,),
        in_specs=attention_specs(total) + [pl.BlockSpec((total, PAIR), lambda i: (0, i))],
        out_specs=[
            pl.BlockSpec((3, total, PAIR), lambda i: (0, 0, i)),
            pl.BlockSpec((None, 2, 2 * total), lambda i: (i, 0, 0)),
        ],
        out_shape=[
            jax.ShapeDtypeStruct((3, total, width), BF16),
            jax.ShapeDtypeStruct((H // 2, 2, 2 * total), F32),
        ],
        compiler_params=pltpu.CompilerParams(vmem_limit_bytes=40 * 2**20),
        cost_estimate=pl.CostEstimate(
            flops=10 * H * total * total * DH * 4, bytes_accessed=16 * total * width,
            transcendentals=H * total * total,
        ),
        name="attend_backward",
    )(rel_pairs, row_seg, col_seg, qkv, qkv, qkv, upstream)


def exchange(blocks_for, place, count, start):
    me = lax.axis_index("shard")
    held = place(start, blocks_for(me), me)
    for step in range(1, count):
        towards = lax.rem(me + step, count)
        source = lax.rem(me + count - step, count)
        pairs = [(i, (i + step) % count) for i in range(count)]
        got = lax.ppermute(blocks_for(towards), "shard", pairs)
        held = place(held, got, source)
    return held


def columns_from_rows(weight, count):
    experts, rows, cols = weight.shape
    part = cols // count

    def block(target):
        return lax.dynamic_slice(weight, (0, 0, target * part), (experts, rows, part))

    def place(held, got, source):
        return lax.dynamic_update_slice(held, got, (0, source * rows, 0))

    return exchange(block, place, count, jnp.zeros((experts, rows * count, part), weight.dtype))


def rows_from_columns(weight, count):
    experts, rows, cols = weight.shape
    part = rows // count

    def block(target):
        return lax.dynamic_slice(weight, (0, target * part, 0), (experts, part, cols))

    def place(held, got, source):
        return lax.dynamic_update_slice(held, got, (0, 0, source * cols))

    return exchange(block, place, count, jnp.zeros((experts, part, cols * count), weight.dtype))


def gather_rows(block):
    return lax.all_gather(block, "shard", axis=0, tiled=True)


def scatter_rows(partial):
    return lax.psum_scatter(partial.astype(BF16), "shard", scatter_dimension=0, tiled=True)


def gelu(value):
    return jax.nn.gelu(value, approximate=True)


def body(
    count,
    tokens,
    cotangent,
    lengths,
    routes,
    buckets,
    w_qkv,
    w_attn_out,
    gains,
    router,
    w_in,
    w_out,
    bias_table,
):
    row_count, width = tokens.shape
    layer_count = w_qkv.shape[0]
    experts = w_in.shape[1]
    slot_count = experts * CAP
    rel_count = buckets.shape[0]

    packed = [w_qkv, w_attn_out[:, None]]
    attn_full = [
        lax.all_gather(
            jnp.concatenate([part[layer] for part in packed], axis=0), "shard", axis=1, tiled=True
        )
        for layer in range(layer_count)
    ]
    small = jnp.concatenate([gains.reshape(-1), router.reshape(-1), bias_table.reshape(-1)])
    small = lax.all_gather(small, "shard", axis=0)
    first, second = gains.size, gains.size + router.size
    own = width // count
    gains_full = (
        small[:, :first]
        .reshape(count, layer_count, 2, own)
        .transpose(1, 2, 0, 3)
        .reshape(layer_count, 2, width)
        .astype(F32)
    )
    router_full = (
        small[:, first:second]
        .reshape(count, layer_count, own, experts)
        .transpose(1, 0, 2, 3)
        .reshape(layer_count, width, experts)
    )
    table_full = small[:, second:].reshape(NB, H).astype(F32)
    inner_full = [columns_from_rows(w_in[layer], count) for layer in range(layer_count)]

    positions = jnp.arange(row_count, dtype=jnp.int32)
    bounds = jnp.cumsum(lengths[0])
    segment = jnp.sum((positions[:, None] >= bounds[None, :]).astype(jnp.int32), axis=1)
    row_seg, col_seg = segment[:, None], segment[None, :]
    live_mask = (positions < bounds[-1]).astype(F32)[:, None]
    bucket_hot = (jnp.arange(NB, dtype=jnp.int32)[:, None] == buckets[None, :]).astype(F32)
    bucket_hot = jnp.pad(bucket_hot, ((0, 0), (0, 2 * row_count - rel_count)))
    rel_pairs = jnp.dot(table_full.T, bucket_hot, precision=HIGHEST).reshape(
        H // 2, 2, 2 * row_count
    )

    def make_plan(layer):
        route = routes[layer, :, 0]
        route_hot = (route[:, None] == jnp.arange(experts, dtype=jnp.int32)[None, :]).astype(
            jnp.int32
        )
        earlier = jnp.cumsum(route_hot, axis=0) - route_hot
        slot_index = route * CAP + jnp.sum(earlier * route_hot, axis=1)
        slots = jnp.arange(slot_count, dtype=jnp.int32)
        placing = (slots[:, None] == slot_index[None, :]).astype(BF16)
        return (placing, route_hot.astype(F32))

    def spread(placing, rows):
        placed = matmul(placing, rows).astype(BF16)
        return [placed[e * CAP : (e + 1) * CAP] for e in range(experts)]

    def collect(placing, parts):
        return matmul(placing, jnp.concatenate(parts, axis=0), ((0,), (0,)))

    hidden = tokens.astype(F32)
    saved = []
    for layer in range(layer_count):
        weights = attn_full[layer]
        placing, route_hot = make_plan(layer)
        scale_one = inverse_rms(hidden)
        normed_one = (hidden * scale_one * gains_full[layer, 0]).astype(BF16)
        qkv = jnp.stack([matmul(normed_one, weights[i]).astype(BF16) for i in range(3)])
        attended = attend_forward(rel_pairs, row_seg, col_seg, qkv)
        middle = hidden + matmul(attended, weights[3])
        scale_two = inverse_rms(middle)
        normed_two = (middle * scale_two * gains_full[layer, 1]).astype(BF16)
        placed = [gather_rows(part) for part in spread(placing, normed_two)]
        logits = matmul(normed_two, router_full[layer])
        shifted = jnp.exp(logits - jnp.max(logits, axis=1, keepdims=True))
        softmax_w = shifted / jnp.sum(shifted, axis=1, keepdims=True)
        gate = jnp.sum(softmax_w * route_hot, axis=1, keepdims=True)
        upward = [matmul(placed[e], inner_full[layer][e]) for e in range(experts)]
        active = [gelu(value).astype(BF16) for value in upward]
        expert_out = [
            scatter_rows(matmul(active[e], w_out[layer, e])) for e in range(experts)
        ]
        combined = collect(placing, expert_out)
        saved.append(
            (
                placing, route_hot, hidden, scale_one, normed_one, qkv, attended, middle,
                scale_two, normed_two, softmax_w, gate, placed, upward, active, combined,
            )
        )
        hidden = middle + gate * combined
    out_tokens = hidden.astype(BF16)

    gradient = cotangent.astype(F32) * live_mask
    attn_grads = [None] * layer_count
    inner_grads = [None] * layer_count
    outer_grads = [None] * layer_count
    gain_grads = [None] * layer_count
    route_grads = [None] * layer_count
    rel_sum = None
    for layer in reversed(range(layer_count)):
        (
            placing, route_hot, hidden, scale_one, normed_one, qkv, attended, middle,
            scale_two, normed_two, softmax_w, gate, placed, upward, active, combined,
        ) = saved[layer]
        weights = attn_full[layer]
        delta_out = [
            gather_rows(part) for part in spread(placing, (gate * gradient).astype(BF16))
        ]
        delta_gate = jnp.sum(gradient * combined, axis=1, keepdims=True)
        delta_logits = (softmax_w * (route_hot - gate) * delta_gate).astype(BF16)
        delta_placed, inner_parts, outer_parts = [], [], []
        for e in range(experts):
            delta_active = matmul(delta_out[e], w_out[layer, e], ((1,), (1,)))
            pull = jax.vjp(gelu, upward[e])[1]
            delta_upward = pull(delta_active)[0].astype(BF16)
            delta_placed.append(
                scatter_rows(matmul(delta_upward, inner_full[layer][e], ((1,), (1,))))
            )
            inner_parts.append(matmul(placed[e], delta_upward, ((0,), (0,))).astype(BF16))
            outer_parts.append(matmul(active[e], delta_out[e], ((0,), (0,))).astype(BF16))
        outer_grads[layer] = lax.psum(jnp.stack(outer_parts), "rep")
        inner_grads[layer] = lax.psum(rows_from_columns(jnp.stack(inner_parts), count), "rep")
        route_grads[layer] = matmul(normed_two, delta_logits, ((0,), (0,)))
        delta_normed_two = collect(placing, delta_placed) + matmul(
            delta_logits, router_full[layer], ((1,), (1,))
        )
        delta_middle, gain_two = norm_backward(
            middle, scale_two, gains_full[layer, 1], delta_normed_two
        )
        delta_middle = delta_middle + gradient
        delta_branch = delta_middle.astype(BF16)
        delta_attended = matmul(delta_branch, weights[3], ((1,), (1,))).astype(BF16)
        delta_qkv, delta_rel = attend_backward(rel_pairs, row_seg, col_seg, qkv, delta_attended)
        rel_sum = delta_rel if rel_sum is None else rel_sum + delta_rel
        projection = [matmul(normed_one, delta_qkv[i], ((0,), (0,))) for i in range(3)]
        projection.append(matmul(attended, delta_branch, ((0,), (0,))))
        attn_part = jnp.stack([part.astype(BF16) for part in projection])
        attn_part = lax.psum_scatter(attn_part, "shard", scatter_dimension=1, tiled=True)
        attn_grads[layer] = lax.psum(attn_part, "rep")
        delta_normed_one = sum(
            matmul(delta_qkv[i], weights[i], ((1,), (1,))) for i in range(3)
        )
        delta_hidden, gain_one = norm_backward(
            hidden, scale_one, gains_full[layer, 0], delta_normed_one
        )
        gradient = delta_hidden + delta_middle
        gain_grads[layer] = jnp.stack([gain_one, gain_two])

    grad_table = jnp.dot(
        bucket_hot, rel_sum.reshape(H, 2 * row_count).T, precision=HIGHEST
    )
    gain_all, route_all = jnp.stack(gain_grads), jnp.stack(route_grads)
    flat = jnp.concatenate([gain_all.reshape(-1), route_all.reshape(-1), grad_table.reshape(-1)])
    flat = lax.psum(flat, ("rep", "shard"))
    first, second = gain_all.size, gain_all.size + route_all.size
    me = lax.axis_index("shard")
    table_rows = NB // count
    grad_gains = lax.dynamic_slice_in_dim(flat[:first].reshape(gain_all.shape), me * own, own, 2)
    grad_router = lax.dynamic_slice_in_dim(
        flat[first:second].reshape(route_all.shape), me * own, own, 1
    )
    grad_table = lax.dynamic_slice_in_dim(
        flat[second:].reshape(NB, H), me * table_rows, table_rows, 0
    )
    attn_all = jnp.stack(attn_grads).astype(F32)
    return (
        out_tokens,
        gradient,
        attn_all[:, :3],
        attn_all[:, 3],
        grad_gains,
        grad_router,
        jnp.stack(inner_grads).astype(F32),
        jnp.stack(outer_grads).astype(F32),
        grad_table,
    )


def solution(mesh):
    rows = P(("rep", "shard"), None)
    weight_specs = (
        P(None, None, "shard", None),
        P(None, "shard", None),
        P(None, None, "shard"),
        P(None, "shard", None),
        P(None, None, "shard", None),
        P(None, None, "shard", None),
        P("shard", None),
    )
    return jax.shard_map(
        functools.partial(body, mesh.shape["shard"]),
        mesh=mesh,
        in_specs=(rows, rows, rows, P(None, ("rep", "shard"), None), P()) + weight_specs,
        out_specs=(rows, rows) + weight_specs,
        check_vma=False,
    )
```
